256 devices in a mesh: depth: 8 (over z_lo, core), row: 4 (over y), col: 8 (over x, z_hi).
Axes of the slice: x: 4, y: 4, z: 8 (z_hi: 2, z_lo: 4; z = z_hi * 4 + z_lo), core: 2. Of those that a mesh axis runs over, the one named last changes fastest.
Arguments:
- x_code: bfloat16 [512, 9216], P(('depth', 'col'), 'row'), may hold values from -4 to 4
- x_scale: float32 [512, 72], P(('depth', 'col'), 'row'), may hold values from 0.3 to 3
- g_code: bfloat16 [512, 9216], P(('depth', 'col'), 'row'), may hold values from -4 to 4
- g_scale: float32 [512, 72], P(('depth', 'col'), 'row'), may hold values from 0.3 to 3
- up_weight: bfloat16 [36864, 9216], P(('depth', 'col'), 'row'), may hold values from -0.0625 to 0.0625
- down_weight: bfloat16 [36864, 9216], P(('depth', 'col'), 'row'), may hold values from -0.03125 to 0.03125
Outputs:
- grad_input: bfloat16 [512, 9216], P(('depth', 'col'), 'row')
- grad_up: bfloat16 [36864, 9216], P(('depth', 'col'), 'row')
- grad_down: bfloat16 [36864, 9216], P(('depth', 'col'), 'row')
The draws below stay inside these ranges and needn't reach their ends.
All inputs are finite; a program needn't handle non-finite values.
Results may differ from the reference program's by a relative error of at most 0.017.
Values may be sent and summed in bfloat16 or wider, within the bound.
No kernel may reach another device: no remote copies, remote signals or barrier semaphores. Data moves between devices by JAX's collectives and lax.ppermute only.
A program may use at most 64 MiB of HBM per device.

```python
import math
import jax
import jax.numpy as jnp
from jax import lax

D = 9216
FF = 36864
TILE = 128
TOKENS = 512


def block_scale(own_key, extent, pieces, low, top_value):
    factor_of = 1.0
    for axis_at, parts in pieces:
        steps = jax.random.uniform(jax.random.fold_in(jax.random.fold_in(own_key, 6), axis_at), (parts,), jnp.float32, low / len(pieces), top_value / len(pieces))
        factor_of = factor_of * jnp.repeat(jnp.exp(steps), extent[axis_at] // parts).reshape((-1,) + (1,) * (len(extent) - 1 - axis_at))
    return factor_of


def scatter_about(rng, dims, scale, most, split=(), kind=jnp.bfloat16):
    factor_of = block_scale(rng, dims, split, -0.22, 0.18) if split else 1.0
    result = jax.random.normal(rng, dims, jnp.float32) * scale * factor_of
    return jnp.minimum(jnp.maximum(result, -most), most).astype(kind)


def setup_inputs(seed: int = 0) -> dict:
    arg_keys = jax.random.split(jax.random.key(seed), 7)
    x_code = scatter_about(arg_keys[0], (TOKENS, D), 1.0, 4.0, ((0, 64), (1, 4)))
    x_scale = jnp.clip(jnp.exp(math.log(3.0) - 2.3025851 * jax.random.uniform(arg_keys[1], (TOKENS, D // TILE), jnp.float32) ** block_scale(arg_keys[1], (TOKENS, D // TILE), ((0, 64), (1, 4)), -0.2, 0.2)), 0.3, 3.0)
    g_code = scatter_about(arg_keys[2], (TOKENS, D), 1.0, 4.0, ((0, 64), (1, 4)))
    g_scale = jnp.clip(jnp.exp(math.log(3.0) - 2.3025851 * jax.random.uniform(arg_keys[3], (TOKENS, D // TILE), jnp.float32) ** block_scale(arg_keys[3], (TOKENS, D // TILE), ((0, 64), (1, 4)), -0.2, 0.2)), 0.3, 3.0)
    up_weight = scatter_about(arg_keys[4], (FF, D), D ** -0.5, 0.0625, ((0, 64), (1, 4)))
    down_weight = scatter_about(arg_keys[5], (FF, D), FF ** -0.5, 0.03125, ((0, 64), (1, 4)))
    return dict(x_code=x_code, x_scale=x_scale, g_code=g_code, g_scale=g_scale, up_weight=up_weight, down_weight=down_weight)


def hadamard():
    indices = jnp.arange(TILE, dtype=jnp.int32)
    common_bits = jnp.bitwise_and(indices[:, None], indices[None, :])
    parity = jnp.zeros((TILE, TILE), jnp.int32)
    for shift_count in range(7):
        parity = parity + jnp.bitwise_and(jnp.right_shift(common_bits, shift_count), 1)
    sign_table = 1 - 2 * jnp.bitwise_and(parity, 1)
    return sign_table.astype(jnp.float32) / math.sqrt(128.0)

def dequant(codes, scales):
    row_count = codes.shape[0]
    col_count = codes.shape[1]
    tiles = codes.astype(jnp.float32).reshape(row_count, col_count // TILE, TILE) * scales[:, :, None]
    turned = jnp.einsum('rki,ij->rkj', tiles, hadamard(), precision=lax.Precision.HIGHEST)
    return turned.reshape(row_count, col_count).astype(jnp.bfloat16)

def reference(x_code, x_scale, g_code, g_scale, up_weight, down_weight):
    inputs = dequant(x_code, x_scale)
    grads = dequant(g_code, g_scale)
    preact = jnp.dot(inputs, up_weight.T, preferred_element_type=jnp.float32)
    grad_act = jnp.dot(grads, down_weight.T, preferred_element_type=jnp.float32)
    positive = jnp.maximum(preact, jnp.float32(0.0))
    squared = (positive * positive).astype(jnp.bfloat16)
    grad_pre = (2.0 * grad_act * positive).astype(jnp.bfloat16)
    grad_down = jnp.dot(squared.T, grads, preferred_element_type=jnp.float32).astype(jnp.bfloat16)
    grad_up = jnp.dot(grad_pre.T, inputs, preferred_element_type=jnp.float32).astype(jnp.bfloat16)
    grad_input = jnp.dot(grad_pre, up_weight, preferred_element_type=jnp.float32).astype(jnp.bfloat16)
    return (grad_input, grad_up, grad_down)
```

```python
import math

import jax
import jax.numpy as jnp
from jax import lax
from jax.experimental import pallas as pl
from jax.experimental.pallas import tpu as pltpu
from jax.sharding import Mesh, PartitionSpec as P

BF = jnp.bfloat16
F32 = jnp.float32
TILE = 128
OFFSETS = (0, -1, -2, -3, -4, 1, 2, 3)
VMEM = 48 * 1024 * 1024


def z_index(z):
    z %= 8
    return (z % 4) * 2 + z // 4


def z_shift(array, k):
    return lax.ppermute(array, ("zl", "zh"), [(z_index(z), z_index(z + k)) for z in range(8)])


def y_shift(array, k):
    return lax.ppermute(array, "y", [(y, (y + k) % 4) for y in range(4)])


def x_from(array, k):
    return lax.ppermute(array, ("y", "x"), [(y * 4 + (x + y + k) % 4, y * 4 + x) for y in range(4) for x in range(4)])


def x_back(array, k):
    return lax.ppermute(array, ("y", "x"), [(y * 4 + x, y * 4 + (x + y + k) % 4) for y in range(4) for x in range(4)])


def other_core(array):
    return lax.ppermute(array, "core", [(0, 1), (1, 0)])


def signs():
    rows = lax.broadcasted_iota(jnp.int32, (TILE, TILE), 0)
    cols = lax.broadcasted_iota(jnp.int32, (TILE, TILE), 1)
    bits = jnp.bitwise_and(rows, cols)
    bits = jnp.bitwise_xor(bits, jnp.right_shift(bits, 4))
    bits = jnp.bitwise_xor(bits, jnp.right_shift(bits, 2))
    bits = jnp.bitwise_xor(bits, jnp.right_shift(bits, 1))
    return (1 - 2 * jnp.bitwise_and(bits, 1)).astype(F32).astype(BF)


def dequant_kernel(xc, xs, gc, gs, inputs, grads):
    tiles = xc.shape[1] // TILE
    codes = [ref[:, k * TILE : (k + 1) * TILE].astype(F32) for ref in (xc, gc) for k in range(tiles)]
    turned = jnp.dot(jnp.concatenate(codes, 0).astype(BF), signs(), preferred_element_type=F32)
    turned = turned * (1.0 / math.sqrt(TILE))
    for at, (scale, out) in enumerate(((xs, inputs), (gs, grads))):
        for k in range(tiles):
            row = (at * tiles + k) * 8
            out[:, k * TILE : (k + 1) * TILE] = (turned[row : row + 8] * scale[:, k : k + 1]).astype(BF)


def dequant(xc, xs, gc, gs):
    shape = jax.ShapeDtypeStruct(xc.shape, BF)
    return pl.pallas_call(dequant_kernel, out_shape=(shape, shape), name="dequant")(xc, xs, gc, gs)


def any_spec():
    return pl.BlockSpec(memory_space=pl.ANY)


def vmem_spec():
    return pl.BlockSpec(memory_space=pltpu.VMEM)


def to_slots(rows):
    return jnp.concatenate([rows[32 * d + 8 * s : 32 * d + 8 * s + 8] for s in range(4) for d in range(8)], 0)


def from_slots(rows):
    return jnp.concatenate([rows[64 * s + 8 * d : 64 * s + 8 * d + 8] for d in range(8) for s in range(4)], 0)


def pre_kernel(*refs):
    i_parts, g_parts, weights = refs[:8], refs[8:12], refs[12:16]
    own, s1, s2, s3, both = refs[16:21]
    i_all, g_all, wu, wd, sems, out_sem = refs[21:]
    copies = []

    def start(src, dst):
        copy = pltpu.make_async_copy(src, dst, sems.at[len(copies)])
        copy.start()
        copies.append(copy)

    hid = weights[0].shape[0]
    start(weights[0], wu.at[pl.ds(0, hid)])
    start(weights[1], wu.at[pl.ds(hid, hid)])
    for n, ref in enumerate(i_parts):
        start(ref, i_all.at[pl.ds(32 * n, 32)])
    first = len(copies)
    start(weights[2], wd.at[pl.ds(0, hid)])
    start(weights[3], wd.at[pl.ds(hid, hid)])
    for n, ref in enumerate(g_parts):
        start(ref, g_all.at[pl.ds(64 * n, 64)])
    outs = (s1, s2, s3)
    step = 384
    for at, (mat, w, lo, hi) in enumerate(((i_all, wu, 0, first), (g_all, wd, first, len(copies)))):
        for copy in copies[lo:hi]:
            copy.wait()
        back = pltpu.make_async_copy(mat, both.at[at], out_sem.at[at])
        back.start()
        for n in range(0, 2 * hid, step):
            part = lax.dot_general(mat[...], w[n : n + step, :], (((1,), (1,)), ((), ())), preferred_element_type=F32)
            if at == 0:
                part = to_slots(part)
            own[at, :, n : n + step] = part[:64]
            for k in range(3):
                outs[k][at, :, n : n + step] = part[64 * (k + 1) : 64 * (k + 2)].astype(BF)
        back.wait()


def pre(i_parts, g_parts, weights):
    hid, wide = weights[0].shape
    sent = jax.ShapeDtypeStruct((2, 64, 2 * hid), BF)
    return pl.pallas_call(
        pre_kernel,
        out_shape=(jax.ShapeDtypeStruct((2, 64, 2 * hid), F32), sent, sent, sent, jax.ShapeDtypeStruct((2, 256, wide), BF)),
        in_specs=[any_spec()] * 16,
        out_specs=[vmem_spec()] * 4 + [any_spec()],
        scratch_shapes=[
            pltpu.VMEM((256, wide), BF),
            pltpu.VMEM((256, wide), BF),
            pltpu.VMEM((2 * hid, wide), BF),
            pltpu.VMEM((2 * hid, wide), BF),
            pltpu.SemaphoreType.DMA((16,)),
            pltpu.SemaphoreType.DMA((2,)),
        ],
        compiler_params=pltpu.CompilerParams(vmem_limit_bytes=VMEM),
        name="pre",
    )(*i_parts, *g_parts, *weights)


def act_kernel(own, r1, r2, r3, out):
    total = [own[at] + r1[at].astype(F32) + r2[at].astype(F32) + r3[at].astype(F32) for at in range(2)]
    positive = jnp.maximum(total[0], 0.0)
    out[0] = (positive * positive).astype(BF)
    out[1] = (2.0 * total[1] * positive).astype(BF)


def act(own, parts):
    return pl.pallas_call(
        act_kernel,
        out_shape=jax.ShapeDtypeStruct(own.shape, BF),
        compiler_params=pltpu.CompilerParams(vmem_limit_bytes=VMEM),
        name="act",
    )(own, *parts)


def back_kernel(p0, p1, p2, p3, w_own, w_oth, o0, o1, o2, o3, keep, send, wu, sems):
    hid = w_own.shape[0]
    c0 = pltpu.make_async_copy(w_own, wu.at[pl.ds(0, hid)], sems.at[0])
    c1 = pltpu.make_async_copy(w_oth, wu.at[pl.ds(hid, hid)], sems.at[1])
    c0.start()
    c1.start()
    parts = (p0, p1, p2, p3)
    for at in range(2):
        full = jnp.concatenate([p[at].astype(F32) for p in parts], 0)
        if at == 1:
            full = from_slots(full)
        full = full.astype(BF)
        keep[at] = full[:, :hid]
        send[at] = full[:, hid:]
    lhs = jnp.concatenate([p[1] for p in parts], 0)
    c0.wait()
    c1.wait()
    step = 768
    for n in range(0, wu.shape[1], step):
        out = jnp.dot(lhs, wu[:, n : n + step], preferred_element_type=F32).astype(BF)
        for k, ref in enumerate((o0, o1, o2, o3)):
            ref[:, n : n + step] = out[64 * k : 64 * k + 64]


def back(parts, w_own, w_oth):
    hid, wide = w_own.shape
    piece = jax.ShapeDtypeStruct((64, wide), BF)
    swap = jax.ShapeDtypeStruct((2, 256, hid), BF)
    return pl.pallas_call(
        back_kernel,
        out_shape=(piece,) * 4 + (swap, swap),
        in_specs=[vmem_spec()] * 4 + [any_spec()] * 2,
        out_specs=[vmem_spec()] * 6,
        scratch_shapes=[pltpu.VMEM((2 * hid, wide), BF), pltpu.SemaphoreType.DMA((2,))],
        compiler_params=pltpu.CompilerParams(vmem_limit_bytes=VMEM),
        name="back",
    )(*parts, w_own, w_oth)


def add_kernel(*refs):
    out = refs[-1]
    total = refs[0][...].astype(F32)
    for ref in refs[1:-1]:
        total = total + ref[...].astype(F32)
    out[...] = total.astype(BF)


def add(*parts):
    return pl.pallas_call(
        add_kernel,
        out_shape=jax.ShapeDtypeStruct(parts[0].shape, BF),
        compiler_params=pltpu.CompilerParams(vmem_limit_bytes=VMEM),
        name="add",
    )(*parts)


def split_kernel(p0, p1, p2, p3, *outs):
    total = p0[...].astype(F32) + p1[...].astype(F32) + p2[...].astype(F32) + p3[...].astype(F32)
    for d, out in enumerate(outs):
        out[...] = total[8 * d : 8 * d + 8].astype(BF)


def add_split(parts):
    return pl.pallas_call(
        split_kernel,
        out_shape=(jax.ShapeDtypeStruct((8, parts[0].shape[1]), BF),) * 8,
        compiler_params=pltpu.CompilerParams(vmem_limit_bytes=VMEM),
        name="add_split",
    )(*parts)


def weights_kernel(keep, came, both, both_came, up, down, sq, gp, mats, sems):
    copies = []
    for at in range(2):
        for half, src in enumerate((both, both_came)):
            copy = pltpu.make_async_copy(src.at[at], mats.at[at, pl.ds(256 * half, 256)], sems.at[at, half])
            copy.start()
            copies.append(copy)
    for at, (ref, out, mat) in enumerate(((sq, down, 1), (gp, up, 0))):
        ref[...] = jnp.concatenate([keep[at], came[at]], 0).T
    for at, (ref, out, mat) in enumerate(((gp, up, 0), (sq, down, 1))):
        copies[2 * mat].wait()
        copies[2 * mat + 1].wait()
        step = 768
        for n in range(0, out.shape[1], step):
            out[:, n : n + step] = jnp.dot(ref[...], mats[mat, :, n : n + step], preferred_element_type=F32).astype(BF)


def weight_grads(keep, came, both, both_came):
    hid, wide = keep.shape[2], both.shape[2]
    shape = jax.ShapeDtypeStruct((hid, wide), BF)
    return pl.pallas_call(
        weights_kernel,
        out_shape=(shape, shape),
        in_specs=[vmem_spec()] * 2 + [any_spec()] * 2,
        out_specs=[vmem_spec()] * 2,
        scratch_shapes=[
            pltpu.VMEM((hid, 512), BF),
            pltpu.VMEM((hid, 512), BF),
            pltpu.VMEM((2, 512, wide), BF),
            pltpu.SemaphoreType.DMA((2, 2)),
        ],
        compiler_params=pltpu.CompilerParams(vmem_limit_bytes=VMEM),
        name="weight_grads",
    )(keep, came, both, both_came)


def gather_z(block):
    right, left = [block], [block]
    for _ in range(3):
        right.append(z_shift(right[-1], 1))
        left.append(z_shift(left[-1], -1))
    right.append(z_shift(right[-1], 1))
    return right + left[1:]


def shards(x_code, x_scale, g_code, g_scale, up_weight, down_weight):
    up_other = other_core(up_weight)
    down_other = other_core(down_weight)
    inputs, grads = dequant(x_code, x_scale, g_code, g_scale)
    i_parts = gather_z(jnp.concatenate([x_from(inputs, k) for k in range(4)], 0))
    column = jnp.concatenate(gather_z(grads), 0)
    g_parts = [x_from(column, k) for k in range(4)]
    own, s1, s2, s3, both = pre(i_parts, g_parts, (up_weight, up_other, down_weight, down_other))
    both_came = other_core(both)
    mine = act(own, [y_shift(s, k) for s, k in ((s1, 1), (s2, 2), (s3, 3))])
    parts = [mine] + [y_shift(mine, -k) for k in (1, 2, 3)]
    *pieces, keep, send = back(parts, up_weight, up_other)
    came = other_core(send)
    blocks = add_split([x_back(piece, k) for k, piece in enumerate(pieces)])
    grad_input = add(*[z_shift(block, dz) if dz else block for block, dz in zip(blocks, OFFSETS)])
    grad_up, grad_down = weight_grads(keep, came, both, both_came)
    return (grad_input, grad_up, grad_down)


def solution(mesh):
    fine = Mesh(mesh.devices.reshape(4, 2, 4, 4, 2), ("zl", "core", "y", "x", "zh"))
    spec = P(("zl", "core", "x", "zh"), "y")
    return jax.shard_map(shards, mesh=fine, in_specs=(spec,) * 6, out_specs=(spec,) * 3, check_vma=False)
```

```python
import functools
import math

import jax
import jax.numpy as jnp
from jax import lax
from jax.experimental import pallas as pl
from jax.experimental.pallas import tpu as pltpu
from jax.sharding import Mesh, PartitionSpec as P

BF = jnp.bfloat16
F32 = jnp.float32
TILE = 128
MIB = 1024 * 1024
NEAR_FIRST = (0, 1, 3, 2)


def on_cores(array, moves):
    def index(z, core):
        z %= 8
        return (z % 4) * 4 + core * 2 + z // 4

    pairs = [(index(z, a), index(z + k, b)) for z in range(8) for a, b, k in moves]
    return lax.ppermute(array, ("zl", "core", "zh"), pairs)


def z_shift(array, k, k1):
    return on_cores(array, ((0, 0, k), (1, 1, k1)))


def xor_shift(array, axis, k):
    return lax.ppermute(array, axis, [(i, i ^ k) for i in range(4)])


def exchange(arrays, axis):
    return [xor_shift(array, axis, k) if k else array for array, k in zip(arrays, NEAR_FIRST)]


def other_core(array):
    return lax.ppermute(array, "core", [(0, 1), (1, 0)])


def in_hbm(*arrays):
    return [pltpu.with_memory_space_constraint(array, pltpu.HBM) for array in arrays]


def in_vmem(array):
    return pltpu.with_memory_space_constraint(array, pltpu.VMEM)


def any_spec():
    return pl.BlockSpec(memory_space=pl.ANY)


def vmem_spec():
    return pl.BlockSpec(memory_space=pltpu.VMEM)


def call(kernel, name, out, operands, ins=None, outs=None, scratch=(), limit=8):
    ins = ins or [False] * len(operands)
    outs = outs or [False] * len(out)
    return pl.pallas_call(
        kernel,
        out_shape=tuple(out),
        in_specs=[any_spec() if a else vmem_spec() for a in ins],
        out_specs=tuple(pl.BlockSpec(memory_space=a) if a else vmem_spec() for a in outs),
        scratch_shapes=list(scratch),
        compiler_params=pltpu.CompilerParams(vmem_limit_bytes=limit * MIB),
        cost_estimate=pl.CostEstimate(flops=1, bytes_accessed=1, transcendentals=0),
        name=name,
    )(*operands)


def struct(*shape, dtype=BF):
    return jax.ShapeDtypeStruct(shape, dtype)


def signs():
    rows = lax.broadcasted_iota(jnp.int32, (TILE, TILE), 0)
    cols = lax.broadcasted_iota(jnp.int32, (TILE, TILE), 1)
    bits = jnp.bitwise_and(rows, cols)
    bits = jnp.bitwise_xor(bits, jnp.right_shift(bits, 4))
    bits = jnp.bitwise_xor(bits, jnp.right_shift(bits, 2))
    bits = jnp.bitwise_xor(bits, jnp.right_shift(bits, 1))
    return (1 - 2 * jnp.bitwise_and(bits, 1)).astype(F32).astype(BF)


def dequant_kernel(xc_in, xs_in, gc_in, gs_in, out, xc, xs, gc, gs, sems):
    copies = [
        pltpu.make_async_copy(src, dst, sems.at[n])
        for n, (src, dst) in enumerate(((xc_in, xc), (gc_in, gc), (xs_in, xs), (gs_in, gs)))
    ]
    for copy in copies:
        copy.start()
    turn = signs()
    for copy in copies:
        copy.wait()
    tiles = xc.shape[1] // TILE
    codes = [ref[:, k * TILE : (k + 1) * TILE].astype(F32) for k in range(tiles) for ref in (xc, gc)]
    turned = jnp.dot(jnp.concatenate(codes, 0).astype(BF), turn, preferred_element_type=F32)
    turned = turned * (1.0 / math.sqrt(TILE))
    for k in range(tiles):
        scale = jnp.concatenate([xs[:, k : k + 1], gs[:, k : k + 1]], 0)
        out[:, k * TILE : (k + 1) * TILE] = (turned[16 * k : 16 * k + 16] * scale).astype(BF)


def regroup_kernel(own, oth, _, inputs, grads):
    own, oth = own[...].astype(F32), oth[...].astype(F32)
    inputs[...] = jnp.concatenate([own[:8], oth[:8]], 0).astype(BF)
    grads[...] = jnp.concatenate([own[8:], oth[8:]], 0).astype(BF)


def first_kernel(x0, x1, x2, x3, g0, g1, _, row, near):
    for n, ref in enumerate((x0, x1, x2, x3)):
        row[n] = ref[...]
    near[0] = g0[...]
    near[1] = g1[...]


def second_kernel(row, row1, near, near1, pair, column):
    pair[0] = row[...]
    pair[1] = row1[...]
    column[:2] = near[...]
    column[2:] = near1[...]


def join_kernel(up_own, up_oth, down_own, down_oth, _, up, down, sems):
    hid = up_own.shape[0]
    copies = []
    for n, (src, dst, at) in enumerate(((up_own, up, 0), (up_oth, up, hid), (down_own, down, 0), (down_oth, down, hid))):
        copies.append(pltpu.make_async_copy(src, dst.at[pl.ds(at, hid)], sems.at[n]))
        copies[-1].start()
    for copy in copies:
        copy.wait()


def pre_kernel(*refs, at, before):
    parts, weights, before, refs = refs[: 2 + 2 * at], refs[2 + 2 * at], refs[3 + 2 * at : 3 + 2 * at + before], refs[3 + 2 * at + before :]
    outs, rows_out, (rows, slots, sems, out_sem) = refs[:4], refs[4], refs[5:]
    y = lax.axis_index("y")
    copies = []
    for n in range(4):
        if at:
            copies.append(pltpu.make_async_copy(parts[n], rows.at[n], sems.at[n]))
        else:
            copies.append(pltpu.make_async_copy(parts[n // 2].at[n % 2], rows.at[:, n], sems.at[n]))
        copies[-1].start()
    for done, out in zip(before, outs):
        out[1 - at] = done[1 - at]
    for copy in copies:
        copy.wait()
    back = pltpu.make_async_copy(rows, rows_out, out_sem)
    back.start()
    hidden, wide = weights.shape
    step = slots.shape[2]
    for n in range(0, hidden, step):
        part = lax.dot_general(
            rows[...].reshape(256, wide), weights[n : n + step, :], (((1,), (1,)), ((), ())), preferred_element_type=F32
        )
        slots[...] = part.reshape(4, 64, step)
        for k, out in zip(NEAR_FIRST, outs):
            out[at, :, n : n + step] = slots[jnp.bitwise_xor(y, k)].astype(out.dtype)
    back.wait()


def pre(parts, weights, at, before):
    hidden, wide = weights.shape
    sent = struct(2, 64, hidden)
    *partial, rows = call(
        functools.partial(pre_kernel, at=at, before=len(before)), "pre",
        [struct(2, 64, hidden, dtype=F32), sent, sent, sent, struct(4, 4, 16, wide)], (*parts, in_vmem(weights), *before),
        ins=[True] * len(parts) + [False] * (1 + len(before)), outs=[False] * 4 + [pl.ANY],
        scratch=[pltpu.VMEM((4, 4, 16, wide), BF), pltpu.VMEM((4, 64, 384), F32), pltpu.SemaphoreType.DMA((4,)), pltpu.SemaphoreType.DMA],
        limit=12,
    )
    return partial, rows


def act_kernel(own, r1, r2, r3, _, __, hidden):
    total = [own[at] + r1[at].astype(F32) + r2[at].astype(F32) + r3[at].astype(F32) for at in range(2)]
    positive = jnp.maximum(total[0], 0.0)
    hidden[0] = (positive * positive).astype(BF)
    hidden[1] = (2.0 * total[1] * positive).astype(BF)


def back_kernel(p0, p1, p2, p3, weights, o0, o1, o2, o3, slots):
    hidden, wide = weights.shape
    y = lax.axis_index("y")
    for k, part in zip(NEAR_FIRST, (p0, p1, p2, p3)):
        slots[jnp.bitwise_xor(y, k)] = part[1]
    step = 768
    for n in range(0, wide, step):
        out = jnp.dot(slots[...].reshape(256, hidden), weights[:, n : n + step], preferred_element_type=F32).astype(BF)
        for k, ref in enumerate((o0, o1, o2, o3)):
            ref[:, n : n + step] = out[64 * k : 64 * k + 64]


def turn_kernel(p0, p1, p2, p3, _, keep, send, slots):
    hid = keep.shape[1]
    y = lax.axis_index("y")
    for k, part in zip(NEAR_FIRST, (p0, p1, p2, p3)):
        slots[jnp.bitwise_xor(y, k)] = part[...]
    for at in range(2):
        turned = slots[:, at].reshape(256, 2 * hid).T
        keep[at] = turned[:hid]
        send[at] = turned[hid:]


def weights_kernel(keep, came, i_own, i_oth, g_own, g_oth, up, down, up_block, down_block, sems):
    hid, wide = up_block.shape
    step = 768
    copies = []
    for at, (own, oth, block, out) in enumerate(((g_own, g_oth, down_block, down), (i_own, i_oth, up_block, up))):
        for i, n in enumerate(range(0, wide, step)):
            cols = pl.ds(n, step)
            total = jnp.dot(keep[at], own[:, :, :, cols].reshape(256, step), preferred_element_type=F32)
            total += jnp.dot(came[at], oth[:, :, :, cols].reshape(256, step), preferred_element_type=F32)
            block[:, cols] = total.astype(BF)
            copies.append(pltpu.make_async_copy(block.at[:, cols], out.at[:, cols], sems.at[at, i]))
            copies[-1].start()
    for copy in copies:
        copy.wait()


def add_kernel(*refs, parts):
    total = refs[0][...].astype(F32)
    for ref in refs[1:parts]:
        total = total + ref[...].astype(F32)
    at = 0
    for out in refs[parts + 1 :]:
        out[...] = total[at : at + out.shape[0]].astype(BF)
        at += out.shape[0]


def add(parts, pieces, after):
    rows, wide = parts[0].shape
    return call(
        functools.partial(add_kernel, parts=len(parts)), "add", [struct(rows // pieces, wide)] * pieces, (*parts, after),
        ins=[False] * len(parts) + [True],
    )


def shards(x_code, x_scale, g_code, g_scale, up_weight, down_weight):
    hid, wide = up_weight.shape
    (mine,) = call(
        dequant_kernel, "dequant", [struct(16, wide)], in_hbm(x_code, x_scale, g_code, g_scale), ins=[True] * 4,
        scratch=[pltpu.VMEM(a.shape, a.dtype) for a in (x_code, x_scale, g_code, g_scale)] + [pltpu.SemaphoreType.DMA((4,))],
    )
    oth = on_cores(mine, ((1, 0, 0), (0, 1, -1)))
    own = on_cores(mine, ((0, 0, 0), (1, 1, -1)))
    up_other = other_core(up_weight)
    down_other = other_core(down_weight)
    inputs, grads = call(regroup_kernel, "regroup", [struct(16, wide)] * 2, (own, oth, up_other), ins=[False] * 2 + [True])
    row, near = call(
        first_kernel, "first", [struct(4, 16, wide), struct(2, 16, wide)],
        (*exchange([inputs] * 4, "x"), grads, z_shift(grads, 1, -1), down_other), ins=[False] * 6 + [True],
    )
    pair, column = call(
        second_kernel, "second", [struct(2, 4, 16, wide), struct(4, 16, wide)], (row, z_shift(row, 1, -1), near, z_shift(near, 2, -2))
    )
    far = z_shift(pair, 2, -2)
    g_parts = exchange([column] * 4, "x")
    up_both, down_both = call(
        join_kernel, "join", [struct(2 * hid, wide)] * 2, (*in_hbm(up_weight, up_other, down_weight, down_other), column),
        ins=[True] * 5, outs=[pl.ANY] * 2, scratch=[pltpu.SemaphoreType.DMA((4,))], limit=1,
    )
    partial, i_rows = pre((pair, far), up_both, 0, ())
    partial, g_rows = pre(g_parts, down_both, 1, partial)
    i_other = other_core(i_rows)
    g_other = other_core(g_rows)
    (hidden,) = call(
        act_kernel, "act", [struct(2, 64, 2 * hid)], (*exchange(partial, "y"), *in_hbm(i_other, g_other)),
        ins=[False] * 4 + [True] * 2,
    )
    hidden = exchange([hidden] * 4, "y")
    pieces = call(
        back_kernel, "back", [struct(64, wide)] * 4, (*hidden, in_vmem(up_both)), scratch=[pltpu.VMEM((4, 64, 2 * hid), BF)], limit=12
    )
    keep, send = call(
        turn_kernel, "turn", [struct(2, hid, 256)] * 2, (*hidden, pieces[0]), ins=[False] * 4 + [True],
        scratch=[pltpu.VMEM((4, 2, 64, 2 * hid), BF)],
    )
    grad_up, grad_down = call(
        weights_kernel, "weight_grads", [struct(hid, wide)] * 2, (keep, other_core(send), i_rows, i_other, g_rows, g_other),
        outs=[pltpu.HBM] * 2, scratch=[pltpu.VMEM((hid, wide), BF), pltpu.VMEM((hid, wide), BF), pltpu.SemaphoreType.DMA((2, 3))],
        limit=24,
    )
    blocks = add(exchange(pieces, "x"), 4, pieces[0])
    home = [z_shift(block, -t, 1 + t) for t, block in enumerate(blocks)]
    half, other_half = add(home, 2, *in_hbm(grad_up))
    (grad_input,) = add([half, other_core(other_half)], 1, half)
    return (grad_input, grad_up, grad_down)


def solution(mesh):
    fine = Mesh(mesh.devices.reshape(4, 2, 4, 4, 2), ("zl", "core", "y", "x", "zh"))
    spec = P(("zl", "core", "x", "zh"), "y")
    return jax.shard_map(shards, mesh=fine, in_specs=(spec,) * 6, out_specs=(spec,) * 3, check_vma=False)
```

```python
import functools
import math

import jax
import jax.numpy as jnp
from jax import lax
from jax.experimental import pallas as pl
from jax.experimental.pallas import tpu as pltpu
from jax.sharding import Mesh, PartitionSpec as P

BF = jnp.bfloat16
F32 = jnp.float32
TILE = 128
MIB = 1024 * 1024
NEAR_FIRST = (0, 1, 3, 2)


def on_cores(array, moves):
    def index(z, core):
        z %= 8
        return (z % 4) * 4 + core * 2 + z // 4

    pairs = [(index(z, a), index(z + k, b)) for z in range(8) for a, b, k in moves]
    return lax.ppermute(array, ("zl", "core", "zh"), pairs)


def z_shift(array, k, k1):
    return on_cores(array, ((0, 0, k), (1, 1, k1)))


def xor_shift(array, axis, k):
    return lax.ppermute(array, axis, [(i, i ^ k) for i in range(4)])


def exchange(arrays, axis):
    return [xor_shift(array, axis, k) if k else array for array, k in zip(arrays, NEAR_FIRST)]


def other_core(array):
    return lax.ppermute(array, "core", [(0, 1), (1, 0)])


def in_hbm(*arrays):
    return [pltpu.with_memory_space_constraint(array, pltpu.HBM) for array in arrays]


def in_vmem(array):
    return pltpu.with_memory_space_constraint(array, pltpu.VMEM)


def any_spec():
    return pl.BlockSpec(memory_space=pl.ANY)


def vmem_spec():
    return pl.BlockSpec(memory_space=pltpu.VMEM)


def call(kernel, name, out, operands, ins=None, outs=None, scratch=(), limit=8):
    ins = ins or [False] * len(operands)
    outs = outs or [False] * len(out)
    return pl.pallas_call(
        kernel,
        out_shape=tuple(out),
        in_specs=[any_spec() if a else vmem_spec() for a in ins],
        out_specs=tuple(pl.BlockSpec(memory_space=a) if a else vmem_spec() for a in outs),
        scratch_shapes=list(scratch),
        compiler_params=pltpu.CompilerParams(vmem_limit_bytes=limit * MIB),
        cost_estimate=pl.CostEstimate(flops=1, bytes_accessed=1, transcendentals=0),
        name=name,
    )(*operands)


def struct(*shape, dtype=BF):
    return jax.ShapeDtypeStruct(shape, dtype)


def signs():
    rows = lax.broadcasted_iota(jnp.int32, (TILE, TILE), 0)
    cols = lax.broadcasted_iota(jnp.int32, (TILE, TILE), 1)
    bits = jnp.bitwise_and(rows, cols)
    bits = jnp.bitwise_xor(bits, jnp.right_shift(bits, 4))
    bits = jnp.bitwise_xor(bits, jnp.right_shift(bits, 2))
    bits = jnp.bitwise_xor(bits, jnp.right_shift(bits, 1))
    return (1 - 2 * jnp.bitwise_and(bits, 1)).astype(F32).astype(BF)


def dequant_kernel(xc_in, xs_in, gc_in, gs_in, out, xc, xs, gc, gs, sems):
    copies = [
        pltpu.make_async_copy(src, dst, sems.at[n])
        for n, (src, dst) in enumerate(((xc_in, xc), (gc_in, gc), (xs_in, xs), (gs_in, gs)))
    ]
    for copy in copies:
        copy.start()
    turn = signs()
    for copy in copies:
        copy.wait()
    tiles = xc.shape[1] // TILE
    codes = [ref[:, k * TILE : (k + 1) * TILE].astype(F32) for k in range(tiles) for ref in (xc, gc)]
    turned = jnp.dot(jnp.concatenate(codes, 0).astype(BF), turn, preferred_element_type=F32)
    turned = turned * (1.0 / math.sqrt(TILE))
    for k in range(tiles):
        scale = jnp.concatenate([xs[:, k : k + 1], gs[:, k : k + 1]], 0)
        out[:, k * TILE : (k + 1) * TILE] = (turned[16 * k : 16 * k + 16] * scale).astype(BF)


def regroup_kernel(own, oth, _, inputs, grads):
    own, oth = own[...].astype(F32), oth[...].astype(F32)
    inputs[...] = jnp.concatenate([own[:8], oth[:8]], 0).astype(BF)
    grads[...] = jnp.concatenate([own[8:], oth[8:]], 0).astype(BF)


def first_kernel(x0, x1, x2, x3, g0, g1, _, row, near):
    for n, ref in enumerate((x0, x1, x2, x3)):
        row[n] = ref[...]
    near[0] = g0[...]
    near[1] = g1[...]


def second_kernel(row, row1, near1, _, __, pair, distant):
    pair[0] = row[...]
    pair[1] = row1[...]
    distant[...] = near1[...]


def join_kernel(up_own, up_oth, down_own, down_oth, _, up, down, sems):
    hid = up_own.shape[0]
    copies = []
    for n, (src, dst, at) in enumerate(((up_own, up, 0), (up_oth, up, hid), (down_own, down, 0), (down_oth, down, hid))):
        copies.append(pltpu.make_async_copy(src, dst.at[pl.ds(at, hid)], sems.at[n]))
        copies[-1].start()
    for copy in copies:
        copy.wait()


def pre_kernel(*refs, parts, at, before):
    parts, weights, before, refs = refs[:parts], refs[parts], refs[parts + 1 : parts + 1 + before], refs[parts + 1 + before :]
    outs, rows_out, (rows, slots, sems, out_sem) = refs[:4], refs[4], refs[5:]
    y = lax.axis_index("y")
    copies = []
    if at:
        for n, ref in enumerate(parts):
            copies.append(pltpu.make_async_copy(ref, rows.at[n % 4, pl.ds(2 * (n // 4), 2)], sems.at[n]))
    else:
        for n in range(4):
            copies.append(pltpu.make_async_copy(parts[n // 2].at[n % 2], rows.at[:, n], sems.at[n]))
    for copy in copies:
        copy.start()
    for done, out in zip(before, outs):
        out[1 - at] = done[1 - at]
    for copy in copies:
        copy.wait()
    back = pltpu.make_async_copy(rows, rows_out, out_sem)
    back.start()
    hidden, wide = weights.shape
    step = slots.shape[2]
    for n in range(0, hidden, step):
        part = lax.dot_general(
            rows[...].reshape(256, wide), weights[n : n + step, :], (((1,), (1,)), ((), ())), preferred_element_type=F32
        )
        slots[...] = part.reshape(4, 64, step)
        for k, out in zip(NEAR_FIRST, outs):
            out[at, :, n : n + step] = slots[jnp.bitwise_xor(y, k)].astype(out.dtype)
    back.wait()


def pre(parts, weights, at, before):
    hidden, wide = weights.shape
    sent = struct(2, 64, hidden)
    *partial, rows = call(
        functools.partial(pre_kernel, parts=len(parts), at=at, before=len(before)), "pre",
        [struct(2, 64, hidden, dtype=F32), sent, sent, sent, struct(4, 4, 16, wide)], (*parts, in_vmem(weights), *before),
        ins=[True] * len(parts) + [False] * (1 + len(before)), outs=[False] * 4 + [pl.ANY],
        scratch=[pltpu.VMEM((4, 4, 16, wide), BF), pltpu.VMEM((4, 64, 384), F32), pltpu.SemaphoreType.DMA((8,)), pltpu.SemaphoreType.DMA],
        limit=12,
    )
    return partial, rows


def act_kernel(own, r1, r2, r3, _, __, squared, grad_pre):
    total = [own[at] + r1[at].astype(F32) + r2[at].astype(F32) + r3[at].astype(F32) for at in range(2)]
    positive = jnp.maximum(total[0], 0.0)
    squared[...] = (positive * positive).astype(BF)
    grad_pre[...] = (2.0 * total[1] * positive).astype(BF)


def back_kernel(p0, p1, p2, p3, weights, o0, o1, o2, o3, slots):
    hidden, wide = weights.shape
    y = lax.axis_index("y")
    for k, part in zip(NEAR_FIRST, (p0, p1, p2, p3)):
        slots[jnp.bitwise_xor(y, k)] = part[...]
    step = 768
    for n in range(0, wide, step):
        out = jnp.dot(slots[...].reshape(256, hidden), weights[:, n : n + step], preferred_element_type=F32).astype(BF)
        for k, ref in enumerate((o0, o1, o2, o3)):
            ref[:, n : n + step] = out[64 * k : 64 * k + 64]


def turn_kernel(*refs):
    parts, keep, send, slots = refs[:8], refs[9], refs[10], refs[11]
    hid = keep.shape[1]
    y = lax.axis_index("y")
    for at in range(2):
        for k, part in zip(NEAR_FIRST, parts[4 * at : 4 * at + 4]):
            slots[at, jnp.bitwise_xor(y, k)] = part[...]
        turned = slots[at].reshape(256, 2 * hid).T
        keep[at] = turned[:hid]
        send[at] = turned[hid:]


def weights_kernel(keep, came, i_own, i_oth, g_own, g_oth, up, down, up_block, down_block, sems):
    hid, wide = up_block.shape
    step = 768
    copies = []
    for at, (own, oth, block, out) in enumerate(((g_own, g_oth, down_block, down), (i_own, i_oth, up_block, up))):
        for i, n in enumerate(range(0, wide, step)):
            cols = pl.ds(n, step)
            total = jnp.dot(keep[at], own[:, :, :, cols].reshape(256, step), preferred_element_type=F32)
            total += jnp.dot(came[at], oth[:, :, :, cols].reshape(256, step), preferred_element_type=F32)
            block[:, cols] = total.astype(BF)
            copies.append(pltpu.make_async_copy(block.at[:, cols], out.at[:, cols], sems.at[at, i]))
            copies[-1].start()
    for copy in copies:
        copy.wait()


def add_kernel(*refs, parts):
    total = refs[0][...].astype(F32)
    for ref in refs[1:parts]:
        total = total + ref[...].astype(F32)
    at = 0
    for out in refs[parts + 1 :]:
        out[...] = total[at : at + out.shape[0]].astype(BF)
        at += out.shape[0]


def add(parts, pieces, after):
    rows, wide = parts[0].shape
    return call(
        functools.partial(add_kernel, parts=len(parts)), "add", [struct(rows // pieces, wide)] * pieces, (*parts, after),
        ins=[False] * len(parts) + [True],
    )


def shards(x_code, x_scale, g_code, g_scale, up_weight, down_weight):
    hid, wide = up_weight.shape
    (mine,) = call(
        dequant_kernel, "dequant", [struct(16, wide)], in_hbm(x_code, x_scale, g_code, g_scale), ins=[True] * 4,
        scratch=[pltpu.VMEM(a.shape, a.dtype) for a in (x_code, x_scale, g_code, g_scale)] + [pltpu.SemaphoreType.DMA((4,))],
    )
    oth = on_cores(mine, ((1, 0, 0), (0, 1, -1)))
    own = on_cores(mine, ((0, 0, 0), (1, 1, -1)))
    up_other = other_core(up_weight)
    down_other = other_core(down_weight)
    inputs, grads = call(regroup_kernel, "regroup", [struct(16, wide)] * 2, (own, oth, up_other), ins=[False] * 2 + [True])
    row, near = call(
        first_kernel, "first", [struct(4, 16, wide), struct(2, 16, wide)],
        (*exchange([inputs] * 4, "x"), grads, z_shift(grads, 1, -1), down_other), ins=[False] * 6 + [True],
    )
    g_near = exchange([near] * 4, "x")
    pair, distant = call(
        second_kernel, "second", [struct(2, 4, 16, wide), struct(2, 16, wide)],
        (row, z_shift(row, 1, -1), z_shift(near, 2, -2), g_near[1], g_near[2]), ins=[False] * 3 + [True] * 2,
    )
    far = z_shift(pair, 2, -2)
    g_distant = exchange([distant] * 4, "x")
    up_both, down_both = call(
        join_kernel, "join", [struct(2 * hid, wide)] * 2, (*in_hbm(up_weight, up_other, down_weight, down_other), row),
        ins=[True] * 5, outs=[pl.ANY] * 2, scratch=[pltpu.SemaphoreType.DMA((4,))], limit=1,
    )
    partial, g_rows = pre((*g_near, *g_distant), down_both, 1, ())
    partial, i_rows = pre((pair, far), up_both, 0, partial)
    i_other = other_core(i_rows)
    g_other = other_core(g_rows)
    squared, grad_pre = call(
        act_kernel, "act", [struct(64, 2 * hid)] * 2, (*exchange(partial, "y"), i_other, g_other),
        ins=[False] * 4 + [True] * 2,
    )
    grad_pre = exchange([grad_pre] * 4, "y")
    squared = exchange([squared] * 4, "y")
    pieces = call(
        back_kernel, "back", [struct(64, wide)] * 4, (*grad_pre, in_vmem(up_both)), scratch=[pltpu.VMEM((4, 64, 2 * hid), BF)], limit=12
    )
    pieces = exchange(pieces, "x")
    blocks = add(pieces, 4, pieces[0])
    home = [z_shift(block, -t, 1 + t) for t, block in enumerate(blocks)]
    keep, send = call(
        turn_kernel, "turn", [struct(2, hid, 256)] * 2, (*squared, *grad_pre, home[0]), ins=[False] * 8 + [True],
        scratch=[pltpu.VMEM((2, 4, 64, 2 * hid), BF)],
    )
    grad_up, grad_down = call(
        weights_kernel, "weight_grads", [struct(hid, wide)] * 2, (keep, other_core(send), i_rows, i_other, g_rows, g_other),
        outs=[pltpu.HBM] * 2, scratch=[pltpu.VMEM((hid, wide), BF), pltpu.VMEM((hid, wide), BF), pltpu.SemaphoreType.DMA((2, 3))],
        limit=24,
    )
    half, other_half = add(home, 2, *in_hbm(grad_up))
    (grad_input,) = add([half, other_core(other_half)], 1, half)
    return (grad_input, grad_up, grad_down)


def solution(mesh):
    fine = Mesh(mesh.devices.reshape(4, 2, 4, 4, 2), ("zl", "core", "y", "x", "zh"))
    spec = P(("zl", "core", "x", "zh"), "y")
    return jax.shard_map(shards, mesh=fine, in_specs=(spec,) * 6, out_specs=(spec,) * 3, check_vma=False)
```

```python
import functools
import math

import jax
import jax.numpy as jnp
from jax import lax
from jax.experimental import pallas as pl
from jax.experimental.pallas import tpu as pltpu
from jax.sharding import Mesh, PartitionSpec as P

BF = jnp.bfloat16
F32 = jnp.float32
TILE = 128
MIB = 1024 * 1024
NEAR_FIRST = (0, 1, 3, 2)


def on_cores(array, moves):
    def index(z, core):
        z %= 8
        return (z % 4) * 4 + core * 2 + z // 4

    pairs = [(index(z, a), index(z + k, b)) for z in range(8) for a, b, k in moves]
    return lax.ppermute(array, ("zl", "core", "zh"), pairs)


def z_shift(array, k, k1):
    return on_cores(array, ((0, 0, k), (1, 1, k1)))


def xor_shift(array, axis, k):
    return lax.ppermute(array, axis, [(i, i ^ k) for i in range(4)])


def exchange(arrays, axis):
    return [xor_shift(array, axis, k) if k else array for array, k in zip(arrays, NEAR_FIRST)]


def other_core(array):
    return lax.ppermute(array, "core", [(0, 1), (1, 0)])


def in_hbm(*arrays):
    return [pltpu.with_memory_space_constraint(array, pltpu.HBM) for array in arrays]


def in_vmem(array):
    return pltpu.with_memory_space_constraint(array, pltpu.VMEM)


def any_spec():
    return pl.BlockSpec(memory_space=pl.ANY)


def vmem_spec():
    return pl.BlockSpec(memory_space=pltpu.VMEM)


def call(kernel, name, out, operands, ins=None, outs=None, scratch=(), limit=8):
    ins = ins or [False] * len(operands)
    outs = outs or [False] * len(out)
    return pl.pallas_call(
        kernel,
        out_shape=tuple(out),
        in_specs=[any_spec() if a else vmem_spec() for a in ins],
        out_specs=tuple(pl.BlockSpec(memory_space=a) if a else vmem_spec() for a in outs),
        scratch_shapes=list(scratch),
        compiler_params=pltpu.CompilerParams(vmem_limit_bytes=limit * MIB),
        cost_estimate=pl.CostEstimate(flops=1, bytes_accessed=1, transcendentals=0),
        name=name,
    )(*operands)


def struct(*shape, dtype=BF):
    return jax.ShapeDtypeStruct(shape, dtype)


def signs():
    rows = lax.broadcasted_iota(jnp.int32, (TILE, TILE), 0)
    cols = lax.broadcasted_iota(jnp.int32, (TILE, TILE), 1)
    bits = jnp.bitwise_and(rows, cols)
    bits = jnp.bitwise_xor(bits, jnp.right_shift(bits, 4))
    bits = jnp.bitwise_xor(bits, jnp.right_shift(bits, 2))
    bits = jnp.bitwise_xor(bits, jnp.right_shift(bits, 1))
    return (1 - 2 * jnp.bitwise_and(bits, 1)).astype(F32).astype(BF)


def dequant_kernel(xc_in, xs_in, gc_in, gs_in, out, xc, xs, gc, gs, sems):
    copies = [
        pltpu.make_async_copy(src, dst, sems.at[n])
        for n, (src, dst) in enumerate(((xc_in, xc), (gc_in, gc), (xs_in, xs), (gs_in, gs)))
    ]
    for copy in copies:
        copy.start()
    turn = signs()
    for copy in copies:
        copy.wait()
    tiles = xc.shape[1] // TILE
    codes = [ref[:, k * TILE : (k + 1) * TILE].astype(F32) for k in range(tiles) for ref in (xc, gc)]
    turned = jnp.dot(jnp.concatenate(codes, 0).astype(BF), turn, preferred_element_type=F32)
    turned = turned * (1.0 / math.sqrt(TILE))
    for k in range(tiles):
        scale = jnp.concatenate([xs[:, k : k + 1], gs[:, k : k + 1]], 0)
        out[:, k * TILE : (k + 1) * TILE] = (turned[16 * k : 16 * k + 16] * scale).astype(BF)


def regroup_kernel(own, oth, _, inputs, grads):
    own, oth = own[...].astype(F32), oth[...].astype(F32)
    inputs[...] = jnp.concatenate([own[:8], oth[:8]], 0).astype(BF)
    grads[...] = jnp.concatenate([own[8:], oth[8:]], 0).astype(BF)


def first_kernel(x0, x1, x2, x3, g0, g1, _, row, near):
    for n, ref in enumerate((x0, x1, x2, x3)):
        row[n] = ref[...]
    near[0] = g0[...]
    near[1] = g1[...]


def second_kernel(row, row1, near1, _, __, pair, distant):
    pair[0] = row[...]
    pair[1] = row1[...]
    distant[...] = near1[...]


def join_kernel(up_own, up_oth, down_own, down_oth, _, up, down, sems):
    hid = up_own.shape[0]
    copies = []
    for n, (src, dst, at) in enumerate(((up_own, up, 0), (up_oth, up, hid), (down_own, down, 0), (down_oth, down, hid))):
        copies.append(pltpu.make_async_copy(src, dst.at[pl.ds(at, hid)], sems.at[n]))
        copies[-1].start()
    for copy in copies:
        copy.wait()


def times(rows, weights, y, slots, outs, at):
    hidden, wide = weights.shape
    step = slots.shape[2]
    for n in range(0, hidden, step):
        part = lax.dot_general(
            rows[...].reshape(256, wide), weights[n : n + step, :], (((1,), (1,)), ((), ())), preferred_element_type=F32
        )
        slots[...] = part.reshape(4, 64, step)
        for k, out in zip(NEAR_FIRST, outs):
            value = slots[jnp.bitwise_xor(y, k)].astype(out.dtype)
            if at is None:
                out[:, n : n + step] = value
            else:
                out[at, :, n : n + step] = value


def grads_kernel(*refs):
    parts, weights, outs, rows, slots = refs[:8], refs[8], refs[9:13], refs[13], refs[14]
    for n, ref in enumerate(parts):
        rows[n % 4, 2 * (n // 4) : 2 * (n // 4) + 2] = ref[...]
    times(rows, weights, lax.axis_index("y"), slots, outs, None)


def inputs_kernel(near, far, weights, g0, g1, g2, g3, g_rows, o0, o1, o2, o3, rows_out, rows, slots):
    for n in range(4):
        rows[:, n] = (near, far)[n // 2][n % 2]
    for done, out in zip((g0, g1, g2, g3), (o0, o1, o2, o3)):
        out[1] = done[...]
    rows_out[0] = rows[...]
    rows_out[1] = g_rows[...]
    times(rows, weights, lax.axis_index("y"), slots, (o0, o1, o2, o3), 0)


def pre(i_parts, g_parts, up, down):
    hidden, wide = up.shape
    rows = struct(4, 4, 16, wide)
    slots = pltpu.VMEM((4, 64, 384), F32)
    *partial, g_rows = call(
        grads_kernel, "grads", [struct(64, hidden, dtype=F32)] + [struct(64, hidden)] * 3 + [rows], (*g_parts, in_vmem(down)),
        scratch=[slots], limit=12,
    )
    *partial, both = call(
        inputs_kernel, "inputs", [struct(2, 64, hidden, dtype=F32)] + [struct(2, 64, hidden)] * 3 + [struct(2, 4, 4, 16, wide)],
        (*i_parts, in_vmem(up), *partial, g_rows), scratch=[pltpu.VMEM((4, 4, 16, wide), BF), slots], limit=12,
    )
    return partial, both


def copy_kernel(src, _, out, sem):
    copy = pltpu.make_async_copy(src, out, sem)
    copy.start()
    copy.wait()


def copied(array, after):
    (out,) = call(
        copy_kernel, "copied", [struct(*array.shape)], (array, after), ins=[True] * 2, outs=[pl.ANY],
        scratch=[pltpu.SemaphoreType.DMA], limit=1,
    )
    return out


def act_kernel(own, r1, r2, r3, squared, grad_pre):
    total = [own[at] + r1[at].astype(F32) + r2[at].astype(F32) + r3[at].astype(F32) for at in range(2)]
    positive = jnp.maximum(total[0], 0.0)
    squared[...] = (positive * positive).astype(BF)
    grad_pre[...] = (2.0 * total[1] * positive).astype(BF)


def back_kernel(p0, p1, p2, p3, weights, o0, o1, o2, o3, slots):
    hidden, wide = weights.shape
    y = lax.axis_index("y")
    for k, part in zip(NEAR_FIRST, (p0, p1, p2, p3)):
        slots[jnp.bitwise_xor(y, k)] = part[...]
    step = 768
    for n in range(0, wide, step):
        out = jnp.dot(slots[...].reshape(256, hidden), weights[:, n : n + step], preferred_element_type=F32).astype(BF)
        for k, ref in enumerate((o0, o1, o2, o3)):
            ref[:, n : n + step] = out[64 * k : 64 * k + 64]


def turn_kernel(*refs):
    parts, keep, send, slots = refs[:8], refs[9], refs[10], refs[11]
    hid = keep.shape[1]
    y = lax.axis_index("y")
    for at in range(2):
        for k, part in zip(NEAR_FIRST, parts[4 * at : 4 * at + 4]):
            slots[at, jnp.bitwise_xor(y, k)] = part[...]
        turned = slots[at].reshape(256, 2 * hid).T
        keep[at] = turned[:hid]
        send[at] = turned[hid:]


def weights_kernel(keep, came, own, oth, up, down, up_block, down_block, sems):
    hid, wide = up_block.shape
    step = 768
    copies = []
    for at, (mat, block, out) in enumerate(((1, down_block, down), (0, up_block, up))):
        for i, n in enumerate(range(0, wide, step)):
            cols = pl.ds(n, step)
            total = jnp.dot(keep[at], own[mat, :, :, :, cols].reshape(256, step), preferred_element_type=F32)
            total += jnp.dot(came[at], oth[mat, :, :, :, cols].reshape(256, step), preferred_element_type=F32)
            block[:, cols] = total.astype(BF)
            copies.append(pltpu.make_async_copy(block.at[:, cols], out.at[:, cols], sems.at[at, i]))
            copies[-1].start()
    for copy in copies:
        copy.wait()


def add_kernel(*refs, parts):
    total = refs[0][...].astype(F32)
    for ref in refs[1:parts]:
        total = total + ref[...].astype(F32)
    at = 0
    for out in refs[parts + 1 :]:
        out[...] = total[at : at + out.shape[0]].astype(BF)
        at += out.shape[0]


def add(parts, pieces, after):
    rows, wide = parts[0].shape
    return call(
        functools.partial(add_kernel, parts=len(parts)), "add", [struct(rows // pieces, wide)] * pieces, (*parts, after),
        ins=[False] * len(parts) + [True],
    )


def shards(x_code, x_scale, g_code, g_scale, up_weight, down_weight):
    hid, wide = up_weight.shape
    (mine,) = call(
        dequant_kernel, "dequant", [struct(16, wide)], in_hbm(x_code, x_scale, g_code, g_scale), ins=[True] * 4,
        scratch=[pltpu.VMEM(a.shape, a.dtype) for a in (x_code, x_scale, g_code, g_scale)] + [pltpu.SemaphoreType.DMA((4,))],
    )
    oth = on_cores(mine, ((1, 0, 0), (0, 1, -1)))
    own = on_cores(mine, ((0, 0, 0), (1, 1, -1)))
    up_other = other_core(up_weight)
    down_other = other_core(down_weight)
    inputs, grads = call(regroup_kernel, "regroup", [struct(16, wide)] * 2, (own, oth, up_other), ins=[False] * 2 + [True])
    row, near = call(
        first_kernel, "first", [struct(4, 16, wide), struct(2, 16, wide)],
        (*exchange([inputs] * 4, "x"), grads, z_shift(grads, 1, -1), down_other), ins=[False] * 6 + [True],
    )
    g_near = exchange([near] * 4, "x")
    pair, distant = call(
        second_kernel, "second", [struct(2, 4, 16, wide), struct(2, 16, wide)],
        (row, z_shift(row, 1, -1), z_shift(near, 2, -2), g_near[1], g_near[2]), ins=[False] * 3 + [True] * 2,
    )
    far = z_shift(pair, 2, -2)
    g_distant = exchange([distant] * 4, "x")
    up_both, down_both = call(
        join_kernel, "join", [struct(2 * hid, wide)] * 2, (*in_hbm(up_weight), in_vmem(up_other), *in_hbm(down_weight), in_vmem(down_other), row),
        ins=[True] * 5, outs=[pl.ANY] * 2, scratch=[pltpu.SemaphoreType.DMA((4,))], limit=1,
    )
    partial, both = pre((pair, far), (*g_near, *g_distant), up_both, down_both)
    squared, grad_pre = call(
        act_kernel, "act", [struct(64, 2 * hid)] * 2, exchange(partial, "y"),
    )
    grad_pre = exchange([grad_pre] * 4, "y")
    squared = exchange([squared] * 4, "y")
    pieces = call(
        back_kernel, "back", [struct(64, wide)] * 4, (*grad_pre, in_vmem(up_both)), scratch=[pltpu.VMEM((4, 64, 2 * hid), BF)], limit=12,
    )
    pieces = exchange(pieces, "x")
    blocks = add(pieces, 4, pieces[0])
    home = [z_shift(block, -t, 1 + t) for t, block in enumerate(blocks)]
    keep, send = call(
        turn_kernel, "turn", [struct(2, hid, 256)] * 2, (*squared, *grad_pre, home[0]), ins=[False] * 8 + [True],
        scratch=[pltpu.VMEM((2, 4, 64, 2 * hid), BF)],
    )
    both_other = other_core(copied(both, keep))
    grad_up, grad_down = call(
        weights_kernel, "weight_grads", [struct(hid, wide)] * 2, (keep, other_core(send), both, both_other),
        outs=[pltpu.HBM] * 2, scratch=[pltpu.VMEM((hid, wide), BF), pltpu.VMEM((hid, wide), BF), pltpu.SemaphoreType.DMA((2, 3))],
        limit=24,
    )
    half, other_half = add(home[:1] + home[:0:-1], 2, *in_hbm(grad_up))
    (grad_input,) = add([half, other_core(other_half)], 1, half)
    return (grad_input, grad_up, grad_down)


def solution(mesh):
    fine = Mesh(mesh.devices.reshape(4, 2, 4, 4, 2), ("zl", "core", "y", "x", "zh"))
    spec = P(("zl", "core", "x", "zh"), "y")
    return jax.shard_map(shards, mesh=fine, in_specs=(spec,) * 6, out_specs=(spec,) * 3, check_vma=False)
```

```python
import functools
import math

import jax
import jax.numpy as jnp
from jax import lax
from jax.experimental import pallas as pl
from jax.experimental.pallas import tpu as pltpu
from jax.sharding import Mesh, PartitionSpec as P

BF = jnp.bfloat16
F32 = jnp.float32
TILE = 128
MIB = 1024 * 1024
NEAR_FIRST = (0, 1, 3, 2)


def on_cores(array, moves):
    def index(z, core):
        z %= 8
        return (z % 4) * 4 + core * 2 + z // 4

    pairs = [(index(z, a), index(z + k, b)) for z in range(8) for a, b, k in moves]
    return lax.ppermute(array, ("zl", "core", "zh"), pairs)


def z_shift(array, k, k1):
    return on_cores(array, ((0, 0, k), (1, 1, k1)))


def xor_shift(array, axis, k):
    return lax.ppermute(array, axis, [(i, i ^ k) for i in range(4)])


def exchange(arrays, axis):
    return [xor_shift(array, axis, k) if k else array for array, k in zip(arrays, NEAR_FIRST)]


def other_core(array):
    return lax.ppermute(array, "core", [(0, 1), (1, 0)])


def in_hbm(*arrays):
    return [pltpu.with_memory_space_constraint(array, pltpu.HBM) for array in arrays]


def in_vmem(array):
    return pltpu.with_memory_space_constraint(array, pltpu.VMEM)


def any_spec():
    return pl.BlockSpec(memory_space=pl.ANY)


def vmem_spec():
    return pl.BlockSpec(memory_space=pltpu.VMEM)


def call(kernel, name, out, operands, ins=None, outs=None, scratch=(), limit=8):
    ins = ins or [False] * len(operands)
    outs = outs or [False] * len(out)
    return pl.pallas_call(
        kernel,
        out_shape=tuple(out),
        in_specs=[any_spec() if a else vmem_spec() for a in ins],
        out_specs=tuple(pl.BlockSpec(memory_space=a) if a else vmem_spec() for a in outs),
        scratch_shapes=list(scratch),
        compiler_params=pltpu.CompilerParams(vmem_limit_bytes=limit * MIB),
        cost_estimate=pl.CostEstimate(flops=1, bytes_accessed=1, transcendentals=0),
        name=name,
    )(*operands)


def struct(*shape, dtype=BF):
    return jax.ShapeDtypeStruct(shape, dtype)


def signs():
    rows = lax.broadcasted_iota(jnp.int32, (TILE, TILE), 0)
    cols = lax.broadcasted_iota(jnp.int32, (TILE, TILE), 1)
    bits = jnp.bitwise_and(rows, cols)
    bits = jnp.bitwise_xor(bits, jnp.right_shift(bits, 4))
    bits = jnp.bitwise_xor(bits, jnp.right_shift(bits, 2))
    bits = jnp.bitwise_xor(bits, jnp.right_shift(bits, 1))
    return (1 - 2 * jnp.bitwise_and(bits, 1)).astype(F32).astype(BF)


def dequant_kernel(xc_in, xs_in, gc_in, gs_in, out, xc, xs, gc, gs, sems):
    copies = [
        pltpu.make_async_copy(src, dst, sems.at[n])
        for n, (src, dst) in enumerate(((xc_in, xc), (gc_in, gc), (xs_in, xs), (gs_in, gs)))
    ]
    for copy in copies:
        copy.start()
    turn = signs()
    for copy in copies:
        copy.wait()
    tiles = xc.shape[1] // TILE
    codes = [ref[:, k * TILE : (k + 1) * TILE].astype(F32) for k in range(tiles) for ref in (xc, gc)]
    turned = jnp.dot(jnp.concatenate(codes, 0).astype(BF), turn, preferred_element_type=F32)
    turned = turned * (1.0 / math.sqrt(TILE))
    for k in range(tiles):
        scale = jnp.concatenate([xs[:, k : k + 1], gs[:, k : k + 1]], 0)
        out[:, k * TILE : (k + 1) * TILE] = (turned[16 * k : 16 * k + 16] * scale).astype(BF)


def regroup_kernel(own, oth, _, inputs, grads):
    own, oth = own[...].astype(F32), oth[...].astype(F32)
    inputs[...] = jnp.concatenate([own[:8], oth[:8]], 0).astype(BF)
    grads[...] = jnp.concatenate([own[8:], oth[8:]], 0).astype(BF)


def first_kernel(x0, x1, x2, x3, g0, g1, _, row, near):
    for n, ref in enumerate((x0, x1, x2, x3)):
        row[n] = ref[...]
    near[0] = g0[...]
    near[1] = g1[...]


def second_kernel(row, row1, near1, _, __, pair, distant):
    pair[0] = row[...]
    pair[1] = row1[...]
    distant[...] = near1[...]


def join_kernel(up_own, up_oth, down_own, down_oth, _, up, down, sems):
    hid = up_own.shape[0]
    copies = []
    for n, (src, dst, at) in enumerate(((up_own, up, 0), (up_oth, up, hid), (down_own, down, 0), (down_oth, down, hid))):
        copies.append(pltpu.make_async_copy(src, dst.at[pl.ds(at, hid)], sems.at[n]))
        copies[-1].start()
    for copy in copies:
        copy.wait()


def times(rows, weights, y, slots, outs, at):
    hidden, wide = weights.shape
    step = slots.shape[2]
    for n in range(0, hidden, step):
        part = lax.dot_general(
            rows[...].reshape(256, wide), weights[n : n + step, :], (((1,), (1,)), ((), ())), preferred_element_type=F32
        )
        slots[...] = part.reshape(4, 64, step)
        for k, out in zip(NEAR_FIRST, outs):
            value = slots[jnp.bitwise_xor(y, k)].astype(out.dtype)
            if at is None:
                out[:, n : n + step] = value
            else:
                out[at, :, n : n + step] = value


def grads_kernel(*refs):
    parts, weights, outs, rows, slots = refs[:8], refs[8], refs[9:13], refs[13], refs[14]
    for n, ref in enumerate(parts):
        rows[n % 4, 2 * (n // 4) : 2 * (n // 4) + 2] = ref[...]
    times(rows, weights, lax.axis_index("y"), slots, outs, None)


def inputs_kernel(near, far, weights, g0, g1, g2, g3, g_rows, o0, o1, o2, o3, rows_out, rows, slots):
    for n in range(4):
        rows[:, n] = (near, far)[n // 2][n % 2]
    for done, out in zip((g0, g1, g2, g3), (o0, o1, o2, o3)):
        out[1] = done[...]
    rows_out[0] = rows[...]
    rows_out[1] = g_rows[...]
    times(rows, weights, lax.axis_index("y"), slots, (o0, o1, o2, o3), 0)


def pre(i_parts, g_parts, up, down):
    hidden, wide = up.shape
    rows = struct(4, 4, 16, wide)
    slots = pltpu.VMEM((4, 64, 384), F32)
    *partial, g_rows = call(
        grads_kernel, "grads", [struct(64, hidden, dtype=F32)] + [struct(64, hidden)] * 3 + [rows], (*g_parts, in_vmem(down)),
        scratch=[slots], limit=12,
    )
    *partial, both = call(
        inputs_kernel, "inputs", [struct(2, 64, hidden, dtype=F32)] + [struct(2, 64, hidden)] * 3 + [struct(2, 4, 4, 16, wide)],
        (*i_parts, in_vmem(up), *partial, g_rows), scratch=[pltpu.VMEM((4, 4, 16, wide), BF), slots], limit=12,
    )
    return partial, both


def copy_kernel(src, _, out, sem):
    copy = pltpu.make_async_copy(src, out, sem)
    copy.start()
    copy.wait()


def copied(array, after):
    (out,) = call(
        copy_kernel, "copied", [struct(*array.shape)], (array, after), ins=[True] * 2, outs=[pl.ANY],
        scratch=[pltpu.SemaphoreType.DMA], limit=1,
    )
    return out


def act_kernel(own, r1, r2, r3, squared, grad_pre):
    total = [own[at] + r1[at].astype(F32) + r2[at].astype(F32) + r3[at].astype(F32) for at in range(2)]
    positive = jnp.maximum(total[0], 0.0)
    squared[...] = (positive * positive).astype(BF)
    grad_pre[...] = (2.0 * total[1] * positive).astype(BF)


def back_kernel(p0, p1, p2, p3, weights, o0, o1, o2, o3, slots):
    hidden, wide = weights.shape
    y = lax.axis_index("y")
    for k, part in zip(NEAR_FIRST, (p0, p1, p2, p3)):
        slots[jnp.bitwise_xor(y, k)] = part[...]
    step = 768
    for n in range(0, wide, step):
        out = jnp.dot(slots[...].reshape(256, hidden), weights[:, n : n + step], preferred_element_type=F32).astype(BF)
        for k, ref in enumerate((o0, o1, o2, o3)):
            ref[:, n : n + step] = out[64 * k : 64 * k + 64]


def turn_kernel(*refs):
    parts, keep, send, slots = refs[:8], refs[9], refs[10], refs[11]
    hid = keep.shape[1]
    y = lax.axis_index("y")
    for at in range(2):
        for k, part in zip(NEAR_FIRST, parts[4 * at : 4 * at + 4]):
            slots[at, jnp.bitwise_xor(y, k)] = part[...]
        turned = slots[at].reshape(256, 2 * hid).T
        keep[at] = turned[:hid]
        send[at] = turned[hid:]


def weights_kernel(keep, came, own, oth, up, down, up_block, down_block, sems):
    hid, wide = up_block.shape
    step = 768
    copies = []
    for at, (mat, block, out) in enumerate(((1, down_block, down), (0, up_block, up))):
        for i, n in enumerate(range(0, wide, step)):
            cols = pl.ds(n, step)
            total = jnp.dot(keep[at], own[mat, :, :, :, cols].reshape(256, step), preferred_element_type=F32)
            total += jnp.dot(came[at], oth[mat, :, :, :, cols].reshape(256, step), preferred_element_type=F32)
            block[:, cols] = total.astype(BF)
            copies.append(pltpu.make_async_copy(block.at[:, cols], out.at[:, cols], sems.at[at, i]))
            copies[-1].start()
    for copy in copies:
        copy.wait()


def add_kernel(*refs, parts):
    total = refs[0][...].astype(F32)
    for ref in refs[1:parts]:
        total = total + ref[...].astype(F32)
    at = 0
    for out in refs[parts + 1 :]:
        out[...] = total[at : at + out.shape[0]].astype(BF)
        at += out.shape[0]


def add(parts, pieces, after):
    rows, wide = parts[0].shape
    return call(
        functools.partial(add_kernel, parts=len(parts)), "add", [struct(rows // pieces, wide)] * pieces, (*parts, after),
        ins=[False] * len(parts) + [True],
    )


def shards(x_code, x_scale, g_code, g_scale, up_weight, down_weight):
    hid, wide = up_weight.shape
    (mine,) = call(
        dequant_kernel, "dequant", [struct(16, wide)], in_hbm(x_code, x_scale, g_code, g_scale), ins=[True] * 4,
        scratch=[pltpu.VMEM(a.shape, a.dtype) for a in (x_code, x_scale, g_code, g_scale)] + [pltpu.SemaphoreType.DMA((4,))],
    )
    oth = on_cores(mine, ((1, 0, 0), (0, 1, -1)))
    own = on_cores(mine, ((0, 0, 0), (1, 1, -1)))
    up_other = other_core(up_weight)
    down_other = other_core(down_weight)
    inputs, grads = call(regroup_kernel, "regroup", [struct(16, wide)] * 2, (own, oth, up_other), ins=[False] * 2 + [True])
    row, near = call(
        first_kernel, "first", [struct(4, 16, wide), struct(2, 16, wide)],
        (*exchange([inputs] * 4, "x"), grads, z_shift(grads, 1, -1), down_other), ins=[False] * 6 + [True],
    )
    g_near = exchange([near] * 4, "x")
    pair, distant = call(
        second_kernel, "second", [struct(2, 4, 16, wide), struct(2, 16, wide)],
        (row, z_shift(row, 1, -1), z_shift(near, 2, -2), g_near[1], g_near[2]), ins=[False] * 3 + [True] * 2,
    )
    far = z_shift(pair, 2, -2)
    g_distant = exchange([distant] * 4, "x")
    up_both, down_both = call(
        join_kernel, "join", [struct(2 * hid, wide)] * 2, (*in_hbm(up_weight), in_vmem(up_other), *in_hbm(down_weight), in_vmem(down_other), row),
        ins=[True] * 5, outs=[pl.ANY] * 2, scratch=[pltpu.SemaphoreType.DMA((4,))], limit=1,
    )
    partial, both = pre((pair, far), (*g_near, *g_distant), up_both, down_both)
    squared, grad_pre = call(
        act_kernel, "act", [struct(64, 2 * hid)] * 2, exchange(partial, "y"),
    )
    grad_pre = exchange([grad_pre] * 4, "y")
    squared = exchange([squared] * 4, "y")
    pieces = call(
        back_kernel, "back", [struct(64, wide)] * 4, (*grad_pre, in_vmem(up_both)), scratch=[pltpu.VMEM((4, 64, 2 * hid), BF)], limit=12,
    )
    pieces = exchange(pieces, "x")
    blocks = add(pieces, 4, pieces[0])
    home = [z_shift(block, -t, 1 + t) for t, block in enumerate(blocks)]
    keep, send = call(
        turn_kernel, "turn", [struct(2, hid, 256)] * 2, (*squared, *grad_pre, blocks[0]), ins=[False] * 8 + [True],
        scratch=[pltpu.VMEM((2, 4, 64, 2 * hid), BF)],
    )
    both_other = other_core(copied(both, keep))
    grad_up, grad_down = call(
        weights_kernel, "weight_grads", [struct(hid, wide)] * 2, (keep, other_core(send), both, both_other),
        outs=[pltpu.HBM] * 2, scratch=[pltpu.VMEM((hid, wide), BF), pltpu.VMEM((hid, wide), BF), pltpu.SemaphoreType.DMA((2, 3))],
        limit=24,
    )
    half, other_half = add(home[:1] + home[:0:-1], 2, *in_hbm(grad_up))
    (grad_input,) = add([half, other_core(other_half)], 1, half)
    return (grad_input, grad_up, grad_down)


def solution(mesh):
    fine = Mesh(mesh.devices.reshape(4, 2, 4, 4, 2), ("zl", "core", "y", "x", "zh"))
    spec = P(("zl", "core", "x", "zh"), "y")
    return jax.shard_map(shards, mesh=fine, in_specs=(spec,) * 6, out_specs=(spec,) * 3, check_vma=False)
```
